32 devices in a mesh: blk: 8 (over y, x, core), freq: 4 (over z).
Axes of the slice: x: 2, y: 2, z: 4, core: 2. Of those that a mesh axis runs over, the one named last changes fastest.
Arguments:
- raw_voltages: bfloat16 [512, 530432], P(('blk', 'freq')), may hold values from -6 to 6
- filter_taps: float32 [4, 2048], replicated, may hold values from -3 to 3
- input_order: int32 [512], P('blk'), may hold values from 0 to 511, as said below
- chan_order: int32 [1024], replicated, may hold values from 0 to 1023, each once
Outputs:
- visibilities: float32 [2, 5, 64, 512, 1024], P(None, None, None, 'blk', 'freq')
The draws below stay inside these ranges and needn't reach their ends.
Inputs may be any that keep to these rules, and one draw needn't show every extreme that they name: input_order is a permutation, and slot k holds a raw input of the same aligned block of 64 slots as k. `chan_order`: each channel once.
All inputs are finite; a program needn't handle non-finite values.
Results may differ from the reference program's by a relative error of at most 0.0029.
Values may be sent and summed in bfloat16 or wider, within the bound.
A program may use at most 256 MiB of HBM per device.

```python
import math
import jax
import jax.numpy as jnp
from jax import lax

INPUTS = 512
CH = 1024
TAPS = 4
SPECTRA = 256
SAMPLES = 530432
TILE = 64
STEPS = 5


def draw_input_order(key, part):
    tile_count = INPUTS // TILE
    scores = jax.random.randint(key, (tile_count, TILE), 0, 1 << 20) * TILE + jnp.arange(TILE, dtype=jnp.int32)[None, :]
    within = jnp.argsort(scores, axis=1, stable=True).astype(jnp.int32)
    starts = (jnp.arange(tile_count, dtype=jnp.int32) * TILE)[:, None]
    return (within + starts).reshape(INPUTS).astype(jnp.int32)


def levels(stream_key, dims, pieces, least, high):
    factor_of = 1.0
    for dim, shards_of in pieces:
        draws = jax.random.uniform(jax.random.fold_in(jax.random.fold_in(stream_key, 6), dim), (shards_of,), jnp.float32, least / len(pieces), high / len(pieces))
        factor_of = factor_of * jnp.repeat(jnp.exp(draws), dims[dim] // shards_of).reshape((-1,) + (1,) * (len(dims) - 1 - dim))
    return factor_of


def noise(own_key, extent, spread, bound, cuts=(), held_as=jnp.bfloat16):
    entries = spread * jax.random.normal(own_key, extent, jnp.float32)
    if cuts:
        entries = entries * levels(own_key, extent, cuts, -0.22, 0.18)
    return jnp.clip(entries, -bound, bound).astype(held_as)


def setup_inputs(seed: int = 0) -> dict:
    seeds = jax.random.split(jax.random.key(seed), 5)
    return {
        "raw_voltages": noise(seeds[0], (INPUTS, SAMPLES), 1.0, 6.0, ((0, 32),)),
        "filter_taps": noise(seeds[1], (TAPS, 2 * CH), TAPS ** -0.5, 3.0, (), jnp.float32),
        "input_order": draw_input_order(jax.random.fold_in(seeds[4], 71), 0),
        "chan_order": jax.random.permutation(seeds[3], CH).astype(jnp.int32),
    }


def make_table(chan_order):
    channel_count = chan_order.shape[0]
    sample_index = jnp.arange(2 * channel_count, dtype=jnp.int32)
    product = sample_index[:, None] * chan_order[None, :] % (2 * channel_count)
    phase_arg = product.astype(jnp.float32) * (math.pi / channel_count)
    return jnp.concatenate([jnp.cos(phase_arg), -jnp.sin(phase_arg)], axis=1) / math.sqrt(channel_count)

def filter_bank(raw_voltages, filter_taps, dft_table):
    input_count = raw_voltages.shape[0]
    channel_count = dft_table.shape[1] // 2
    frames = raw_voltages.astype(jnp.float32).reshape(input_count, SPECTRA + TAPS - 1, 2 * channel_count)
    filtered = filter_taps[0] * frames[:, 0:SPECTRA]
    for tap_index in range(1, TAPS):
        filtered = filtered + filter_taps[tap_index] * frames[:, tap_index:tap_index + SPECTRA]
    transformed = jnp.dot(filtered.reshape(input_count * SPECTRA, 2 * channel_count), dft_table, precision=lax.Precision.HIGHEST)
    transformed = transformed.reshape(input_count, SPECTRA, 2, channel_count).transpose(0, 2, 1, 3)
    return transformed.astype(jnp.bfloat16)

def reference(raw_voltages, filter_taps, input_order, chan_order):
    dft_table = make_table(chan_order)
    tile_count = INPUTS // TILE
    blocks = raw_voltages.reshape(tile_count, TILE, SAMPLES)
    spectra = lax.map(lambda block: filter_bank(block, filter_taps, dft_table), blocks)
    spectra = spectra.reshape(INPUTS, 2, SPECTRA, CH)
    slotted = spectra[input_order.astype(jnp.int32)]
    tile_blocks = slotted.reshape(tile_count, TILE, 2, SPECTRA, CH)
    plain = tile_blocks.reshape(tile_count, TILE, 2 * SPECTRA, CH).astype(jnp.float32)
    rotated = jnp.concatenate([tile_blocks[:, :, 1], -tile_blocks[:, :, 0]], axis=2).astype(jnp.float32)
    results = []
    for offset in range(STEPS):
        partners = jnp.roll(plain, offset, axis=0)
        vis_real = jnp.einsum('bjtc,bitc->jbic', partners, plain) / SPECTRA
        vis_imag = jnp.einsum('bjtc,bitc->jbic', partners, rotated) / SPECTRA
        results.append(jnp.stack([vis_real.reshape(TILE, INPUTS, CH), vis_imag.reshape(TILE, INPUTS, CH)]))
    return jnp.stack(results, axis=1)
```

```python
import math

import jax
import jax.numpy as jnp
from jax import lax
from jax.sharding import PartitionSpec as P

TAPS = 4
SPECTRA = 256


def make_table(chan_rows, channel_count):
    sample_count = 2 * channel_count
    fine = 32

    def turn(samples):
        product = samples * chan_rows[..., None] % sample_count
        phase = product.astype(jnp.float32) * (math.pi / channel_count)
        return jnp.cos(phase), jnp.sin(phase)

    coarse_cos, coarse_sin = turn(jnp.arange(sample_count // fine, dtype=jnp.int32) * fine)
    fine_cos, fine_sin = turn(jnp.arange(fine, dtype=jnp.int32))
    coarse_cos, coarse_sin = coarse_cos[..., :, None], coarse_sin[..., :, None]
    fine_cos, fine_sin = fine_cos[..., None, :], fine_sin[..., None, :]
    scale = 1.0 / math.sqrt(channel_count)
    whole = chan_rows.shape + (sample_count,)
    real = ((coarse_cos * fine_cos - coarse_sin * fine_sin) * scale).reshape(whole)
    imag = ((coarse_sin * fine_cos + coarse_cos * fine_sin) * -scale).reshape(whole)
    return jnp.stack([real, imag], axis=1)


def per_device(raw_voltages, filter_taps, input_order, chan_order):
    blk, freq = lax.axis_size("blk"), lax.axis_size("freq")
    count = blk * freq
    held = raw_voltages.shape[0]
    channel_count = chan_order.shape[0]
    width = channel_count // count
    tile = input_order.shape[0]
    inputs = held * count
    offsets = blk // 2 + 1

    order = lax.all_gather(input_order, "blk", tiled=True)
    rows = chan_order.reshape(freq, blk, width).transpose(1, 0, 2).reshape(count, width)
    table = make_table(rows, channel_count)

    frames = raw_voltages.reshape(held, SPECTRA + TAPS - 1, 2 * channel_count)
    filtered = filter_taps[0] * frames[:, 0:SPECTRA].astype(jnp.float32)
    for tap in range(1, TAPS):
        filtered = filtered + filter_taps[tap] * frames[:, tap : tap + SPECTRA].astype(jnp.float32)
    spectra = jnp.einsum(
        "drkm,itm->drkit", table, filtered, precision=lax.Precision.HIGH
    ).astype(jnp.bfloat16)
    turned = lax.all_to_all(spectra, ("blk", "freq"), 0, 0, tiled=True)

    by_channel = turned.transpose(2, 1, 0, 3, 4).reshape(width, 2, inputs, SPECTRA)
    chosen = (order[:, None] == jnp.arange(inputs, dtype=jnp.int32)[None, :]).astype(jnp.bfloat16)
    chosen = jnp.broadcast_to(chosen, (width,) + chosen.shape)
    parts = [
        jnp.einsum(
            "kpi,kit->kpt", chosen, by_channel[:, part], preferred_element_type=jnp.float32
        ).astype(jnp.bfloat16)
        for part in range(2)
    ]
    plain = jnp.concatenate(parts, axis=2)
    rotated = jnp.concatenate([parts[1], -parts[0]], axis=2)
    around = jnp.concatenate([plain[:, inputs - (offsets - 1) * tile :], plain], axis=1)
    blocks = []
    for b in range(blk):
        own = slice(b * tile, (b + 1) * tile)
        both = jnp.concatenate([plain[:, own], rotated[:, own]], axis=1)
        partners = around[:, b * tile : (b + offsets) * tile]
        product = jnp.einsum("kpt,kit->kpi", partners, both, preferred_element_type=jnp.float32)
        blocks.append((product * (1.0 / SPECTRA)).astype(jnp.bfloat16))
    sent = jnp.stack(blocks)
    arrived = lax.all_to_all(sent, "blk", 0, 0, tiled=True)
    arrived = arrived.reshape(blk * width, offsets, tile, 2, tile)
    return jnp.flip(arrived, axis=1).transpose(3, 1, 2, 4, 0).astype(jnp.float32)


def solution(mesh):
    placed = (P(("blk", "freq"), None), P(), P("blk"), P())
    return jax.shard_map(
        per_device,
        mesh=mesh,
        in_specs=placed,
        out_specs=P(None, None, None, "blk", "freq"),
        check_vma=False,
    )
```
